512 devices in a mesh: row: 16 (over y_lo, x, core), col: 32 (over z, y_hi).
Axes of the slice: x: 4, y: 8 (y_hi: 4, y_lo: 2; y = y_hi * 2 + y_lo), z: 8, core: 2. Of those that a mesh axis runs over, the one named last changes fastest.
Arguments:
- ginv_top: bfloat16 [8192, 8192], P('col', 'row'), may hold values from -6 to 6
- panel_one: bfloat16 [8192, 2048], P(('row', 'col')), may hold values from -0.09375 to 0.09375
- panel_two: bfloat16 [8192, 4096], P(('row', 'col')), may hold values from -0.125 to 0.125
- parent_link: bfloat16 [2048, 1024], P('row'), may hold values from -0.25 to 0.25
- dinv_one: bfloat16 [512, 2048], P('col', 'row'), may hold values from -6 to 6
- struct_one: int32 [4, 8], replicated, may hold values from 0 to 15, as said below
- struct_two: int32 [8, 4], replicated, may hold values from 0 to 15, as said below
Outputs:
- ginv_one: bfloat16 [8192, 2048], P('col', 'row')
- diag_one: bfloat16 [512, 2048], P('col', 'row')
- ginv_two: bfloat16 [4096, 8192], P('row', 'col')
The draws below stay inside these ranges and needn't reach their ends.
Inputs may be any that keep to these rules, and one draw needn't show every extreme that they name: `struct_one`: each row lists 8 distinct ancestor block indices in rising order; every row holds 15, and row 0 holds 0. `struct_two`: row q lists 4 distinct indices in rising order, all taken from row q // 2 of struct_one; row 0 holds 0 and row 1 holds 15.
All inputs are finite; a program needn't handle non-finite values.
Results may differ from the reference program's by a relative error of at most 0.02.
Values may be sent and summed in bfloat16 or wider, within the bound.
No kernel may reach another device: no remote copies, remote signals or barrier semaphores. Data moves between devices by JAX's collectives and lax.ppermute only.
A program may use at most 64 MiB of HBM per device.

```python
import jax
import jax.numpy as jnp
from jax import lax

B = 512
NA = 16
LEVEL1 = 4
LEVEL2 = 8
S1 = 8
S2 = 4
N_ROW = 16


def shared_pattern(key):
    first_key, second_key = jax.random.split(key)
    block_ids = jnp.arange(NA, dtype=jnp.int32)
    jitter = jax.random.randint(first_key, (LEVEL1, NA), 0, NA, dtype=jnp.int32)
    scores = (jitter + block_ids[None, :]) * NA + block_ids[None, :]
    forced = jnp.zeros((LEVEL1, NA), jnp.int32).at[:, NA - 1].set(4 * NA * NA).at[0, 0].set(4 * NA * NA)
    _, chosen = lax.top_k(scores + forced, S1)
    struct_one = jnp.sort(chosen, axis=1).astype(jnp.int32)
    parents = struct_one[jnp.arange(LEVEL2, dtype=jnp.int32) // 2]
    slots = jnp.arange(S1, dtype=jnp.int32)
    jitter_two = jax.random.randint(second_key, (LEVEL2, S1), 0, S1, dtype=jnp.int32)
    scores_two = jitter_two * S1 + slots[None, :]
    scores_two = scores_two.at[0, 0].add(4 * S1 * S1).at[1, S1 - 1].add(4 * S1 * S1)
    _, picked = lax.top_k(scores_two, S2)
    struct_two = jnp.sort(jnp.take_along_axis(parents, picked, axis=1), axis=1).astype(jnp.int32)
    return (struct_one, struct_two)


def draw_struct_one(key, part):
    return shared_pattern(key)[0]


def draw_struct_two(key, part):
    return shared_pattern(key)[1]


def block_levels(own_key, extent, shards, least, top_value):
    level, own = 1.0, jax.random.fold_in(own_key, 6)
    for position, parts in shards:
        steps = jnp.exp(jax.random.uniform(jax.random.fold_in(own, position), (parts,), jnp.float32, least / len(shards), top_value / len(shards)))
        level = level * jnp.repeat(steps, extent[position] // parts).reshape([-1 if axis == position else 1 for axis in range(len(extent))])
    return level


def bell_draw(own_key, shape, scale, bound, shards=(), held_as=jnp.bfloat16):
    values = scale * jax.random.normal(own_key, shape, jnp.float32)
    if shards:
        values = values * block_levels(own_key, shape, shards, -0.22, 0.18)
    return jnp.clip(values, -bound, bound).astype(held_as)


def setup_inputs(seed: int = 0) -> dict:
    streams_of = jax.random.split(jax.random.key(seed), 8)
    return {
        "ginv_top": bell_draw(streams_of[0], (NA * B, NA * B), 1.0, 6.0, ((0, 32), (1, 16))),
        "panel_one": bell_draw(streams_of[1], (NA * B, LEVEL1 * B), (S1 * B) ** -0.5, 0.09375, ((0, 512),)),
        "panel_two": bell_draw(streams_of[2], (NA * B, LEVEL2 * B), (S2 * B) ** -0.5, 0.125, ((0, 512),)),
        "parent_link": bell_draw(streams_of[3], (LEVEL1 * B, 2 * B), B ** -0.5, 0.25, ((0, 16),)),
        "dinv_one": bell_draw(streams_of[4], (B, LEVEL1 * B), 1.0, 6.0, ((0, 32), (1, 16))),
        "struct_one": draw_struct_one(jax.random.fold_in(streams_of[7], 71), 0),
        "struct_two": draw_struct_two(jax.random.fold_in(streams_of[7], 71), 0),
    }


def reference(ginv_top, panel_one, panel_two, parent_link, dinv_one, struct_one, struct_two):
    block_ids = jnp.arange(NA, dtype=jnp.int32)
    hit_one = jnp.any(struct_one[:, :, None] == block_ids[None, None, :], axis=1)
    hit_two = jnp.any(struct_two[:, :, None] == block_ids[None, None, :], axis=1)
    keep_one = jnp.repeat(jnp.repeat(hit_one.T, B, axis=0), B, axis=1)
    keep_two = jnp.repeat(jnp.repeat(hit_two.T, B, axis=0), B, axis=1)
    lm_one = jnp.where(keep_one, panel_one, jnp.zeros_like(panel_one))
    lm_two = jnp.where(keep_two, panel_two, jnp.zeros_like(panel_two))
    slab_size = NA * B // N_ROW

    def add_one(index, running):
        top_cols = lax.dynamic_slice_in_dim(ginv_top, index * slab_size, slab_size, 1)
        panel_rows = lax.dynamic_slice_in_dim(lm_one, index * slab_size, slab_size, 0)
        rounded = jnp.dot(top_cols, panel_rows, preferred_element_type=jnp.float32).astype(jnp.bfloat16)
        rounded = lax.optimization_barrier(rounded)
        return running + rounded.astype(jnp.float32)

    start_one = jnp.zeros((NA * B, LEVEL1 * B), jnp.float32)
    ginv_one = (-lax.fori_loop(0, N_ROW, add_one, start_one)).astype(jnp.bfloat16)

    diag_terms = jnp.einsum("iqb,iqc->bqc", lm_one.reshape(NA * B, LEVEL1, B).astype(jnp.float32),
                            ginv_one.reshape(NA * B, LEVEL1, B).astype(jnp.float32))
    diag_one = (dinv_one.astype(jnp.float32) - diag_terms.reshape(B, LEVEL1 * B)).astype(jnp.bfloat16)

    link_blocks = parent_link.reshape(LEVEL1, B, 2 * B)
    identity = jnp.eye(LEVEL1, dtype=jnp.bfloat16)
    link_full = (link_blocks[:, :, None, :] * identity[:, None, :, None]).reshape(LEVEL1 * B, LEVEL2 * B)
    slab_width = LEVEL1 * B // N_ROW
    dims = (((0,), (1,)), ((), ()))

    def add_two(index, running):
        top_cols = lax.dynamic_slice_in_dim(ginv_top, index * slab_size, slab_size, 1)
        panel_rows = lax.dynamic_slice_in_dim(lm_two, index * slab_size, slab_size, 0)
        direct = lax.dot_general(panel_rows, top_cols, dims, preferred_element_type=jnp.float32)
        link_rows = lax.dynamic_slice_in_dim(link_full, index * slab_width, slab_width, 0)
        upper_cols = lax.dynamic_slice_in_dim(ginv_one, index * slab_width, slab_width, 1)
        through = lax.dot_general(link_rows, upper_cols, dims, preferred_element_type=jnp.float32)
        rounded = (direct + through).astype(jnp.bfloat16)
        rounded = lax.optimization_barrier(rounded)
        return running + rounded.astype(jnp.float32)

    start_two = jnp.zeros((LEVEL2 * B, NA * B), jnp.float32)
    ginv_two = (-lax.fori_loop(0, N_ROW, add_two, start_two)).astype(jnp.bfloat16)
    return ginv_one, diag_one, ginv_two
```

```python
import functools

import jax
import jax.numpy as jnp
from jax import lax
from jax.experimental import pallas as pl
from jax.experimental.pallas import tpu as pltpu
from jax.sharding import Mesh, PartitionSpec as P

ROW = ("ylo", "xh", "xl", "core")
COL = ("z", "yhi")
GROUP = ("xl", "core")
F32 = jnp.float32
BF16 = jnp.bfloat16
VMEM_LIMIT = 40 * 1024 * 1024


def params():
    return pltpu.CompilerParams(vmem_limit_bytes=VMEM_LIMIT)


def pack_kernel(idx, x_ref, out_ref):
    for s in range(8):
        out_ref[s] = x_ref[idx[s], :, 0:128]
    for s in range(4):
        block = idx[8 + s]
        out_ref[8 + 2 * s] = x_ref[block, :, 128:256]
        out_ref[9 + 2 * s] = x_ref[block, :, 256:384]


def pack(idx, x):
    return pl.pallas_call(
        pack_kernel,
        out_shape=jax.ShapeDtypeStruct((16, 16, 128), BF16),
        grid_spec=pltpu.PrefetchScalarGridSpec(
            num_scalar_prefetch=1,
            grid=(1,),
            in_specs=[pl.BlockSpec((16, 16, 384), lambda i, idx: (0, 0, 0))],
            out_specs=pl.BlockSpec((16, 16, 128), lambda i, idx: (0, 0, 0)),
        ),
        compiler_params=params(),
        name="pack",
    )(idx, x)


def upper_kernel(idx, g_ref, *refs):
    blocks = refs[:8]
    out_ref, own_ref = refs[8:10]
    panel, acc = refs[10:]
    s = pl.program_id(0)

    @pl.when(s == 0)
    def _():
        z = idx[12]
        for d in range(8):
            place = pl.multiple_of(lax.rem(z + 8 - d, 8) * 64, 64)
            for slot in range(8):
                for y in range(4):
                    panel[slot, pl.ds(place + y * 16, 16), :] = blocks[d][y, slot]
        acc[...] = jnp.zeros_like(acc)
        half = pl.multiple_of(idx[13] * 256, 256)
        rows = panel[idx[14], pl.ds(half, 256), :]
        own_ref[...] = jnp.where(idx[15] > 0, rows, jnp.zeros_like(rows))

    acc[...] += jnp.dot(g_ref[0], panel[s], preferred_element_type=F32)

    @pl.when(s == 7)
    def _():
        out_ref[...] = (-acc[...]).astype(BF16)


def upper(idx, g_all, blocks):
    whole = pl.BlockSpec((4, 8, 16, 128), lambda s, idx: (0, 0, 0, 0))
    flat = pl.BlockSpec((256, 128), lambda s, idx: (0, 0))
    return pl.pallas_call(
        upper_kernel,
        out_shape=(
            jax.ShapeDtypeStruct((256, 128), BF16),
            jax.ShapeDtypeStruct((256, 128), BF16),
        ),
        grid_spec=pltpu.PrefetchScalarGridSpec(
            num_scalar_prefetch=1,
            grid=(8,),
            in_specs=[pl.BlockSpec((1, 256, 512), lambda s, idx: (idx[s], 0, 0))] + [whole] * 8,
            out_specs=(flat, flat),
            scratch_shapes=[pltpu.VMEM((8, 512, 128), BF16), pltpu.VMEM((256, 128), F32)],
        ),
        compiler_params=params(),
        cost_estimate=pl.CostEstimate(
            flops=2 * 256 * 4096 * 128, bytes_accessed=3 * 1024 * 1024, transcendentals=0
        ),
        name="upper",
    )(idx, g_all, *blocks)


def cross_kernel(idx, lm_ref, gone_ref, link_ref, part_ref, *t_refs):
    gone = gone_ref[...]
    for h in range(4):
        part = lax.dot_general(
            lm_ref[h], gone, (((0,), (0,)), ((), ())), preferred_element_type=F32
        )
        part_ref[pl.ds(h * 128, 128), :] = part.astype(BF16)
    member = idx[16]
    for m in range(4):
        start = pl.multiple_of(jnp.bitwise_xor(member, m) * 256, 256)
        link = link_ref[:, pl.ds(start, 256)]
        term = jnp.dot(gone, link, preferred_element_type=F32)
        t_refs[m][...] = term.T.astype(BF16)


def cross(idx, lm, gone, link):
    term = pl.BlockSpec((256, 256), lambda i, idx: (0, 0))
    return pl.pallas_call(
        cross_kernel,
        out_shape=(jax.ShapeDtypeStruct((512, 128), BF16),)
        + (jax.ShapeDtypeStruct((256, 256), BF16),) * 4,
        grid_spec=pltpu.PrefetchScalarGridSpec(
            num_scalar_prefetch=1,
            grid=(1,),
            in_specs=[
                pl.BlockSpec((4, 256, 128), lambda i, idx: (0, 0, 0)),
                pl.BlockSpec((256, 128), lambda i, idx: (0, 0)),
                pl.BlockSpec((128, 1024), lambda i, idx: (0, 0)),
            ],
            out_specs=(pl.BlockSpec((512, 128), lambda i, idx: (0, 0)),) + (term,) * 4,
        ),
        compiler_params=params(),
        name="cross",
    )(idx, lm, gone, link)


def lower_kernel(idx, g_ref, m_ref, t0, t1, t2, t3, out_ref, acc):
    s = pl.program_id(0)

    @pl.when(s == 0)
    def _():
        acc[...] = jnp.zeros_like(acc)

    g = g_ref[0]
    for h in range(2):
        cols = m_ref[:, :, h].reshape(512, 128)
        acc[h] += jnp.dot(g, cols, preferred_element_type=F32)

    @pl.when(s == 3)
    def _():
        for h in range(2):
            rows = pl.ds(h * 128, 128)
            total = acc[h].T
            for t in (t0, t1, t2, t3):
                total += t[rows, :].astype(F32)
            out_ref[rows, :] = (-total).astype(BF16)


def lower(idx, g_all, m_two, terms):
    flat = pl.BlockSpec((256, 256), lambda s, idx: (0, 0))
    return pl.pallas_call(
        lower_kernel,
        out_shape=jax.ShapeDtypeStruct((256, 256), BF16),
        grid_spec=pltpu.PrefetchScalarGridSpec(
            num_scalar_prefetch=1,
            grid=(4,),
            in_specs=[
                pl.BlockSpec((1, 256, 512), lambda s, idx: (idx[8 + s], 0, 0)),
                pl.BlockSpec((8, 4, 2, 16, 128), lambda s, idx: (0, 0, s, 0, 0)),
            ]
            + [flat] * 4,
            out_specs=flat,
            scratch_shapes=[pltpu.VMEM((2, 256, 128), F32)],
        ),
        compiler_params=params(),
        cost_estimate=pl.CostEstimate(
            flops=2 * 256 * 2048 * 256, bytes_accessed=2 * 1024 * 1024, transcendentals=0
        ),
        name="lower",
    )(idx, g_all, m_two, *terms)


def per_device(ginv_top, panel_one, panel_two, parent_link, dinv_one, struct_one, struct_two):
    r = lax.axis_index(ROW)
    c = lax.axis_index(COL)
    z = lax.axis_index("z")
    member = lax.axis_index(GROUP)
    list_one = lax.dynamic_index_in_dim(struct_one, r // 4, 0, keepdims=False)
    list_two = lax.dynamic_index_in_dim(struct_two, r // 2, 0, keepdims=False)
    own = list_one == c // 2
    idx = jnp.concatenate(
        [
            list_one,
            list_two,
            jnp.stack([z, c % 2, jnp.argmax(own), jnp.any(own), member]).astype(jnp.int32),
        ]
    )

    g_all = lax.all_gather(ginv_top, ROW, axis=0, tiled=False)

    slots = jnp.concatenate(
        [panel_one.reshape(16, 16, 128), panel_two.reshape(16, 16, 256)], axis=2
    ).transpose(1, 0, 2)
    mine = lax.all_to_all(slots, ROW, 0, 0)
    packed = pack(idx, mine)
    across = lax.all_gather(packed, "yhi", axis=0, tiled=False)
    up_block, down_block = across[:, :8], across[:, 8:]

    m_two = lax.all_gather(down_block, "z", axis=0, tiled=False)

    up = [(i, (i + 1) % 8) for i in range(8)]
    down = [(i, (i - 1) % 8) for i in range(8)]
    blocks = [up_block] + [None] * 7
    a = b = up_block
    for s in range(1, 5):
        a = lax.ppermute(a, "z", up)
        blocks[s] = a
        if s < 4:
            b = lax.ppermute(b, "z", down)
            blocks[8 - s] = b

    ginv_one, own_rows = upper(idx, g_all, blocks)
    lm = lax.all_gather(own_rows, GROUP, axis=0, tiled=False)
    part, t0, t1, t2, t3 = cross(idx, lm, ginv_one, parent_link)
    t1 = lax.ppermute(t1, GROUP, [(i, i ^ 1) for i in range(4)])
    t2 = lax.ppermute(t2, GROUP, [(i, i ^ 2) for i in range(4)])
    t3 = lax.ppermute(t3, GROUP, [(i, i ^ 3) for i in range(4)])

    parts = lax.all_to_all(part.reshape(32, 16, 128), COL, 0, 0)
    diag_sum = jnp.sum(parts.astype(F32), axis=0)
    diag_one = (dinv_one.astype(F32) - diag_sum).astype(BF16)

    ginv_two = lower(idx, g_all, m_two, (t0, t1, t2, t3))
    return (ginv_one, diag_one, ginv_two)


def solution(mesh):
    fine = Mesh(mesh.devices.reshape(2, 2, 2, 2, 8, 4), ROW + COL)
    return jax.shard_map(
        per_device,
        mesh=fine,
        in_specs=(
            P(COL, ROW),
            P(ROW + COL, None),
            P(ROW + COL, None),
            P(ROW, None),
            P(COL, ROW),
            P(),
            P(),
        ),
        out_specs=(P(COL, ROW), P(COL, ROW), P(ROW, COL)),
        check_vma=False,
    )
```

```python
import functools

import jax
import jax.numpy as jnp
from jax import lax
from jax.experimental import pallas as pl
from jax.experimental.pallas import tpu as pltpu
from jax.sharding import Mesh, PartitionSpec as P

ROW = ("ylo", "xh", "xl", "core")
COL = ("z", "yhi")
GROUP = ("xl", "core")
F32 = jnp.float32
BF16 = jnp.bfloat16
VMEM_LIMIT = 40 * 1024 * 1024


def params():
    return pltpu.CompilerParams(vmem_limit_bytes=VMEM_LIMIT)


def pack_kernel(idx, x_ref, out_ref):
    for s in range(8):
        out_ref[s] = x_ref[idx[s], :, 0:128]
    for s in range(4):
        block = idx[8 + s]
        out_ref[8 + 2 * s] = x_ref[block, :, 128:256]
        out_ref[9 + 2 * s] = x_ref[block, :, 256:384]


def pack(idx, x):
    return pl.pallas_call(
        pack_kernel,
        out_shape=jax.ShapeDtypeStruct((16, 16, 128), BF16),
        grid_spec=pltpu.PrefetchScalarGridSpec(
            num_scalar_prefetch=1,
            grid=(1,),
            in_specs=[pl.BlockSpec((16, 16, 384), lambda i, idx: (0, 0, 0))],
            out_specs=pl.BlockSpec((16, 16, 128), lambda i, idx: (0, 0, 0)),
        ),
        compiler_params=params(),
        name="pack",
    )(idx, x)


def upper_kernel(idx, g_ref, m_ref, near_ref, out_ref, acc):
    s = pl.program_id(0)

    @pl.when(s == 0)
    def _():
        acc[...] = jnp.zeros_like(acc)
        rows = near_ref[...].reshape(256, 128)
        out_ref[1] = jnp.where(idx[15] > 0, rows, jnp.zeros_like(rows))

    acc[...] += jnp.dot(g_ref[0], m_ref[...].reshape(512, 128), preferred_element_type=F32)

    @pl.when(s == 7)
    def _():
        out_ref[0] = (-acc[...]).astype(BF16)


def upper(idx, g_all, m_one):
    return pl.pallas_call(
        upper_kernel,
        out_shape=jax.ShapeDtypeStruct((2, 256, 128), BF16),
        grid_spec=pltpu.PrefetchScalarGridSpec(
            num_scalar_prefetch=1,
            grid=(8,),
            in_specs=[
                pl.BlockSpec((1, 256, 512), lambda s, idx: (idx[s], 0, 0)),
                pl.BlockSpec((8, 4, 1, 16, 128), lambda s, idx: (0, 0, s, 0, 0)),
                pl.BlockSpec((4, 4, 1, 16, 128), lambda s, idx: (idx[13], 0, idx[14], 0, 0)),
            ],
            out_specs=pl.BlockSpec((2, 256, 128), lambda s, idx: (0, 0, 0)),
            scratch_shapes=[pltpu.VMEM((256, 128), F32)],
        ),
        compiler_params=params(),
        cost_estimate=pl.CostEstimate(
            flops=2 * 256 * 4096 * 128, bytes_accessed=3 * 1024 * 1024, transcendentals=0
        ),
        name="upper",
    )(idx, g_all, m_one, m_one)


def cross_kernel(pair_ref, mine_ref, part_ref):
    gone = mine_ref[0]
    for h in range(4):
        part = lax.dot_general(
            pair_ref[h, 1], gone, (((0,), (0,)), ((), ())), preferred_element_type=F32
        )
        part_ref[pl.ds(h * 128, 128), :] = part.astype(BF16)


def cross(pairs, mine):
    return pl.pallas_call(
        cross_kernel,
        out_shape=jax.ShapeDtypeStruct((512, 128), BF16),
        compiler_params=params(),
        name="cross",
    )(pairs, mine)


def lower_kernel(idx, g_ref, m_ref, pair_ref, l0, l1, l2, l3, out_ref, acc):
    s = pl.program_id(0)

    @pl.when(s == 0)
    def _():
        member = idx[16]
        total = jnp.zeros((256, 256), F32)
        for m, link in enumerate((l0, l1, l2, l3)):
            gone = pair_ref[jnp.bitwise_xor(member, m), 0]
            total += jnp.dot(gone, link[...], preferred_element_type=F32)
        acc[0] = total[:, 0:128]
        acc[1] = total[:, 128:256]

    g = g_ref[0]
    for h in range(2):
        cols = m_ref[:, :, h].reshape(512, 128)
        acc[h] += jnp.dot(g, cols, preferred_element_type=F32)

    @pl.when(s == 3)
    def _():
        for h in range(2):
            out_ref[pl.ds(h * 128, 128), :] = (-acc[h].T).astype(BF16)


def lower(idx, g_all, m_two, pairs, links):
    flat = pl.BlockSpec((128, 256), lambda s, idx: (0, 0))
    return pl.pallas_call(
        lower_kernel,
        out_shape=jax.ShapeDtypeStruct((256, 256), BF16),
        grid_spec=pltpu.PrefetchScalarGridSpec(
            num_scalar_prefetch=1,
            grid=(4,),
            in_specs=[
                pl.BlockSpec((1, 256, 512), lambda s, idx: (idx[8 + s], 0, 0)),
                pl.BlockSpec((8, 4, 2, 16, 128), lambda s, idx: (0, 0, s, 0, 0)),
                pl.BlockSpec((4, 2, 256, 128), lambda s, idx: (0, 0, 0, 0)),
            ]
            + [flat] * 4,
            out_specs=pl.BlockSpec((256, 256), lambda s, idx: (0, 0)),
            scratch_shapes=[pltpu.VMEM((2, 256, 128), F32)],
        ),
        compiler_params=params(),
        cost_estimate=pl.CostEstimate(
            flops=2 * 256 * 2560 * 256, bytes_accessed=3 * 1024 * 1024, transcendentals=0
        ),
        name="lower",
    )(idx, g_all, m_two, pairs, *links)


def settle_kernel(dinv_ref, parts_ref, out_ref):
    total = jnp.sum(parts_ref[...].astype(F32), axis=0)
    out_ref[...] = (dinv_ref[...].astype(F32) - total).astype(BF16)


def settle(dinv, parts):
    return pl.pallas_call(
        settle_kernel,
        out_shape=jax.ShapeDtypeStruct((16, 128), BF16),
        compiler_params=params(),
        name="settle",
    )(dinv, parts)


def per_device(ginv_top, panel_one, panel_two, parent_link, dinv_one, struct_one, struct_two):
    r = lax.axis_index(ROW)
    c = lax.axis_index(COL)
    z = lax.axis_index("z")
    member = lax.axis_index(GROUP)
    list_one = lax.dynamic_index_in_dim(struct_one, r // 4, 0, keepdims=False)
    list_two = lax.dynamic_index_in_dim(struct_two, r // 2, 0, keepdims=False)
    own = list_one == c // 2
    idx = jnp.concatenate(
        [
            list_one,
            list_two,
            jnp.stack([z, c % 2, jnp.argmax(own), jnp.any(own), member]).astype(jnp.int32),
        ]
    )

    g_all = lax.all_gather(ginv_top, ROW, axis=0, tiled=False)

    slots = jnp.concatenate(
        [panel_one.reshape(16, 16, 128), panel_two.reshape(16, 16, 256)], axis=2
    ).transpose(1, 0, 2)
    mine = lax.all_to_all(slots, ROW, 0, 0)

    packed = pack(idx, mine)
    across = lax.all_gather(packed, "yhi", axis=0, tiled=False)
    up_block, down_block = across[:, :8], across[:, 8:]
    copies = jnp.broadcast_to(up_block, (8, 4, 8, 16, 128))

    copies, parent_link = lax.optimization_barrier((copies, parent_link))
    m_one = lax.all_to_all(copies, "z", 0, 0)
    links = []
    for m in range(4):
        to = jnp.bitwise_xor(member, m)
        link = lax.dynamic_slice_in_dim(parent_link, to * 256, 256, 1)
        if m:
            link = lax.ppermute(link, GROUP, [(i, i ^ m) for i in range(4)])
        links.append(link)
    g_all, down_block, *links = lax.optimization_barrier((g_all, down_block, *links))
    m_two = lax.all_gather(down_block, "z", axis=0, tiled=False)

    mine_one = upper(idx, g_all, m_one)
    pairs = lax.all_gather(mine_one, GROUP, axis=0, tiled=False)
    part = cross(pairs, mine_one)
    parts = lax.all_to_all(part.reshape(32, 16, 128), COL, 0, 0)
    diag_one = settle(dinv_one, parts)

    ginv_two = lower(idx, g_all, m_two, pairs, links)
    return (mine_one[0], diag_one, ginv_two)


def solution(mesh):
    fine = Mesh(mesh.devices.reshape(2, 2, 2, 2, 8, 4), ROW + COL)
    return jax.shard_map(
        per_device,
        mesh=fine,
        in_specs=(
            P(COL, ROW),
            P(ROW + COL, None),
            P(ROW + COL, None),
            P(ROW, None),
            P(COL, ROW),
            P(),
            P(),
        ),
        out_specs=(P(COL, ROW), P(COL, ROW), P(ROW, COL)),
        check_vma=False,
    )
```

```python
import functools

import jax
import jax.numpy as jnp
from jax import lax
from jax.experimental import pallas as pl
from jax.experimental.pallas import tpu as pltpu
from jax.sharding import Mesh, PartitionSpec as P

ROW = ("ylo", "xh", "xl", "core")
COL = ("z", "yhi")
GROUP = ("xl", "core")
F32 = jnp.float32
BF16 = jnp.bfloat16
VMEM_LIMIT = 24 * 1024 * 1024


def params():
    return pltpu.CompilerParams(vmem_limit_bytes=VMEM_LIMIT)


def pack_kernel(idx, x_ref, out_ref):
    for s in range(8):
        out_ref[s] = x_ref[idx[s], :, 0:128]
    for s in range(4):
        block = idx[17 + s]
        out_ref[8 + 2 * s] = x_ref[block, :, 128:256]
        out_ref[9 + 2 * s] = x_ref[block, :, 256:384]


def pack(idx, x):
    return pl.pallas_call(
        pack_kernel,
        out_shape=jax.ShapeDtypeStruct((16, 16, 128), BF16),
        grid_spec=pltpu.PrefetchScalarGridSpec(
            num_scalar_prefetch=1,
            grid=(1,),
            in_specs=[pl.BlockSpec((16, 16, 384), lambda i, idx: (0, 0, 0))],
            out_specs=pl.BlockSpec((16, 16, 128), lambda i, idx: (0, 0, 0)),
        ),
        compiler_params=params(),
        name="pack",
    )(idx, x)


def choose_kernel(idx, g_ref, out_ref, sem):
    copies = [pltpu.make_async_copy(g_ref.at[idx[s]], out_ref.at[s], sem.at[s]) for s in range(8)]
    for copy in copies:
        copy.start()
    for copy in copies:
        copy.wait()


def choose(idx, g_all):
    return pl.pallas_call(
        choose_kernel,
        out_shape=jax.ShapeDtypeStruct((8, 256, 512), BF16),
        grid_spec=pltpu.PrefetchScalarGridSpec(
            num_scalar_prefetch=1,
            grid=(1,),
            in_specs=[pl.BlockSpec(memory_space=pl.ANY)],
            out_specs=pl.BlockSpec(memory_space=pl.ANY),
            scratch_shapes=[pltpu.SemaphoreType.DMA((8,))],
        ),
        compiler_params=params(),
        name="choose",
    )(idx, g_all)


def whole(shape):
    return pl.BlockSpec(shape, lambda i, idx: (0,) * len(shape))


def upper_kernel(idx, g_ref, m_ref, out_ref):
    rows = m_ref[pl.ds(idx[13] * 4, 4), :, idx[14]].reshape(256, 128)
    out_ref[1] = jnp.where(idx[15] > 0, rows, jnp.zeros_like(rows))
    acc = jnp.zeros((256, 128), F32)
    for s in range(8):
        cols = m_ref[:, :, s].reshape(512, 128)
        acc += jnp.dot(g_ref[s], cols, preferred_element_type=F32)
    out_ref[0] = (-acc).astype(BF16)


def upper(idx, g_own, m_one):
    return pl.pallas_call(
        upper_kernel,
        out_shape=jax.ShapeDtypeStruct((2, 256, 128), BF16),
        grid_spec=pltpu.PrefetchScalarGridSpec(
            num_scalar_prefetch=1,
            grid=(1,),
            in_specs=[whole((8, 256, 512)), whole((8, 4, 8, 16, 128))],
            out_specs=whole((2, 256, 128)),
        ),
        compiler_params=params(),
        cost_estimate=pl.CostEstimate(
            flops=2 * 256 * 4096 * 128, bytes_accessed=3 * 1024 * 1024, transcendentals=0
        ),
        name="upper",
    )(idx, g_own, m_one)


def cross_kernel(pair_ref, mine_ref, part_ref):
    gone = mine_ref[0]
    for h in range(4):
        part = lax.dot_general(
            pair_ref[h, 1], gone, (((0,), (0,)), ((), ())), preferred_element_type=F32
        )
        part_ref[pl.ds(h * 128, 128), :] = part.astype(BF16)


def cross(pairs, mine):
    return pl.pallas_call(
        cross_kernel,
        out_shape=jax.ShapeDtypeStruct((512, 128), BF16),
        compiler_params=params(),
        name="cross",
    )(pairs, mine)


def through_kernel(idx, pair_ref, l0, l1, l2, l3, out_ref):
    member = idx[16]
    for h in range(2):
        acc = jnp.zeros((256, 128), F32)
        for m, link in enumerate((l0, l1, l2, l3)):
            gone = pair_ref[jnp.bitwise_xor(member, m), 0]
            cols = link[:, h * 128 : (h + 1) * 128]
            acc += jnp.dot(gone, cols, preferred_element_type=F32)
        out_ref[h] = acc


def through(idx, pairs, links):
    return pl.pallas_call(
        through_kernel,
        out_shape=jax.ShapeDtypeStruct((2, 256, 128), F32),
        grid_spec=pltpu.PrefetchScalarGridSpec(
            num_scalar_prefetch=1,
            grid=(1,),
            in_specs=[whole((4, 2, 256, 128))] + [whole((128, 256))] * 4,
            out_specs=whole((2, 256, 128)),
        ),
        compiler_params=params(),
        name="through",
    )(idx, pairs, *links)


def lower_kernel(idx, g_ref, m_ref, add_ref, out_ref):
    for h in range(2):
        acc = add_ref[h]
        for s in range(4):
            cols = m_ref[:, :, 2 * s + h].reshape(512, 128)
            acc += jnp.dot(g_ref[idx[8 + s]], cols, preferred_element_type=F32)
        out_ref[h * 128 : (h + 1) * 128, :] = (-acc.T).astype(BF16)


def lower(idx, g_own, m_two, add):
    return pl.pallas_call(
        lower_kernel,
        out_shape=jax.ShapeDtypeStruct((256, 256), BF16),
        grid_spec=pltpu.PrefetchScalarGridSpec(
            num_scalar_prefetch=1,
            grid=(1,),
            in_specs=[
                whole((8, 256, 512)),
                whole((8, 4, 8, 16, 128)),
                whole((2, 256, 128)),
            ],
            out_specs=whole((256, 256)),
        ),
        compiler_params=params(),
        cost_estimate=pl.CostEstimate(
            flops=2 * 256 * 2048 * 256, bytes_accessed=3 * 1024 * 1024, transcendentals=0
        ),
        name="lower",
    )(idx, g_own, m_two, add)


def settle_kernel(dinv_ref, parts_ref, out_ref):
    total = jnp.sum(parts_ref[...].astype(F32), axis=0)
    out_ref[...] = (dinv_ref[...].astype(F32) - total).astype(BF16)


def settle(dinv, parts):
    return pl.pallas_call(
        settle_kernel,
        out_shape=jax.ShapeDtypeStruct((16, 128), BF16),
        compiler_params=params(),
        name="settle",
    )(dinv, parts)


def per_device(ginv_top, panel_one, panel_two, parent_link, dinv_one, struct_one, struct_two):
    r = lax.axis_index(ROW)
    c = lax.axis_index(COL)
    z = lax.axis_index("z")
    member = lax.axis_index(GROUP)
    list_one = lax.dynamic_index_in_dim(struct_one, r // 4, 0, keepdims=False)
    list_two = lax.dynamic_index_in_dim(struct_two, r // 2, 0, keepdims=False)
    own = list_one == c // 2
    place_two = jnp.argmax(list_one[None, :] == list_two[:, None], axis=1)
    here = jnp.stack([z, c % 2, jnp.argmax(own), jnp.any(own), member])
    idx = jnp.concatenate(
        [list_one, place_two.astype(jnp.int32), here.astype(jnp.int32), list_two]
    )

    g_all = lax.all_gather(ginv_top, ROW, axis=0, tiled=False)

    slots = jnp.concatenate(
        [panel_one.reshape(16, 16, 128), panel_two.reshape(16, 16, 256)], axis=2
    ).transpose(1, 0, 2)
    mine = lax.all_to_all(slots, ROW, 0, 0)

    packed = pack(idx, mine)
    across = lax.all_gather(packed, "yhi", axis=0, tiled=False)
    up_block, down_block = across[:, :8], across[:, 8:]
    copies = jnp.broadcast_to(up_block, (8, 4, 8, 16, 128))

    copies, parent_link = lax.optimization_barrier((copies, parent_link))
    m_one = lax.all_to_all(copies, "z", 0, 0)
    links = []
    for m in range(4):
        to = jnp.bitwise_xor(member, m)
        link = lax.dynamic_slice_in_dim(parent_link, to * 256, 256, 1)
        if m:
            link = lax.ppermute(link, GROUP, [(i, i ^ m) for i in range(4)])
        links.append(link)
    g_all, down_block, *links = lax.optimization_barrier((g_all, down_block, *links))
    m_two = lax.all_gather(down_block, "z", axis=0, tiled=False)
    g_own = choose(idx, g_all)
    m_one, g_own = lax.optimization_barrier((m_one, g_own))

    mine_one = upper(idx, g_own, m_one)
    pairs = lax.all_gather(mine_one, GROUP, axis=0, tiled=False)
    part = cross(pairs, mine_one)
    parts = lax.all_to_all(part.reshape(32, 16, 128), COL, 0, 0)
    diag_one = settle(dinv_one, parts)

    ginv_two = lower(idx, g_own, m_two, through(idx, pairs, links))
    return (mine_one[0], diag_one, ginv_two)


def solution(mesh):
    fine = Mesh(mesh.devices.reshape(2, 2, 2, 2, 8, 4), ROW + COL)
    return jax.shard_map(
        per_device,
        mesh=fine,
        in_specs=(
            P(COL, ROW),
            P(ROW + COL, None),
            P(ROW + COL, None),
            P(ROW, None),
            P(COL, ROW),
            P(),
            P(),
        ),
        out_specs=(P(COL, ROW), P(COL, ROW), P(ROW, COL)),
        check_vma=False,
    )
```

```python
import functools

import jax
import jax.numpy as jnp
from jax import lax
from jax.experimental import pallas as pl
from jax.experimental.pallas import tpu as pltpu
from jax.sharding import Mesh, PartitionSpec as P

ROW = ("ylo", "xh", "xl", "core")
COL = ("z", "yhi")
GROUP = ("xl", "core")
F32 = jnp.float32
BF16 = jnp.bfloat16
VMEM_LIMIT = 24 * 1024 * 1024


def params():
    return pltpu.CompilerParams(vmem_limit_bytes=VMEM_LIMIT)


def pack_kernel(idx, x_ref, out_ref):
    for s in range(8):
        out_ref[s] = x_ref[idx[s], :, 0:128]
    for s in range(4):
        block = idx[17 + s]
        out_ref[8 + 2 * s] = x_ref[block, :, 128:256]
        out_ref[9 + 2 * s] = x_ref[block, :, 256:384]


def pack(idx, x):
    return pl.pallas_call(
        pack_kernel,
        out_shape=jax.ShapeDtypeStruct((16, 16, 128), BF16),
        grid_spec=pltpu.PrefetchScalarGridSpec(
            num_scalar_prefetch=1,
            grid=(1,),
            in_specs=[pl.BlockSpec((16, 16, 384), lambda i, idx: (0, 0, 0))],
            out_specs=pl.BlockSpec((16, 16, 128), lambda i, idx: (0, 0, 0)),
        ),
        compiler_params=params(),
        name="pack",
    )(idx, x)


def choose_kernel(idx, g_ref, out_ref, sem):
    copies = [pltpu.make_async_copy(g_ref.at[idx[s]], out_ref.at[s], sem.at[s]) for s in range(8)]
    for copy in copies:
        copy.start()
    for copy in copies:
        copy.wait()


def choose(idx, g_all):
    return pl.pallas_call(
        choose_kernel,
        out_shape=jax.ShapeDtypeStruct((8, 256, 512), BF16),
        grid_spec=pltpu.PrefetchScalarGridSpec(
            num_scalar_prefetch=1,
            grid=(1,),
            in_specs=[pl.BlockSpec(memory_space=pl.ANY)],
            out_specs=pl.BlockSpec(memory_space=pl.ANY),
            scratch_shapes=[pltpu.SemaphoreType.DMA((8,))],
        ),
        compiler_params=params(),
        name="choose",
    )(idx, g_all)


def whole(shape):
    return pl.BlockSpec(shape, lambda i, idx: (0,) * len(shape))


def upper_kernel(idx, g_ref, m_ref, out_ref):
    rows = m_ref[pl.ds(idx[13] * 4, 4), :, idx[14]].reshape(256, 128)
    out_ref[1] = jnp.where(idx[15] > 0, rows, jnp.zeros_like(rows))
    acc = jnp.zeros((256, 128), F32)
    for s in range(8):
        cols = m_ref[:, :, s].reshape(512, 128)
        acc += jnp.dot(g_ref[s], cols, preferred_element_type=F32)
    out_ref[0] = (-acc).astype(BF16)


def upper(idx, g_own, m_one):
    return pl.pallas_call(
        upper_kernel,
        out_shape=jax.ShapeDtypeStruct((2, 256, 128), BF16),
        grid_spec=pltpu.PrefetchScalarGridSpec(
            num_scalar_prefetch=1,
            grid=(1,),
            in_specs=[whole((8, 256, 512)), whole((8, 4, 8, 16, 128))],
            out_specs=whole((2, 256, 128)),
        ),
        compiler_params=params(),
        cost_estimate=pl.CostEstimate(
            flops=2 * 256 * 4096 * 128, bytes_accessed=3 * 1024 * 1024, transcendentals=0
        ),
        name="upper",
    )(idx, g_own, m_one)


def cross_kernel(pair_ref, mine_ref, part_ref):
    gone = mine_ref[0]
    for h in range(4):
        part = lax.dot_general(
            pair_ref[h, 1], gone, (((0,), (0,)), ((), ())), preferred_element_type=F32
        )
        part_ref[pl.ds(h * 128, 128), :] = part.astype(BF16)


def cross(pairs, mine):
    return pl.pallas_call(
        cross_kernel,
        out_shape=jax.ShapeDtypeStruct((512, 128), BF16),
        compiler_params=params(),
        name="cross",
    )(pairs, mine)


def through_kernel(idx, pair_ref, l0, l1, l2, l3, out_ref):
    member = idx[16]
    acc = jnp.zeros((256, 256), F32)
    for m, link in enumerate((l0, l1, l2, l3)):
        gone = pair_ref[jnp.bitwise_xor(member, m), 0]
        acc += jnp.dot(gone, link[...], preferred_element_type=F32)
    out_ref[...] = acc


def through(idx, pairs, links):
    return pl.pallas_call(
        through_kernel,
        out_shape=jax.ShapeDtypeStruct((256, 256), F32),
        grid_spec=pltpu.PrefetchScalarGridSpec(
            num_scalar_prefetch=1,
            grid=(1,),
            in_specs=[whole((4, 2, 256, 128))] + [whole((128, 256))] * 4,
            out_specs=whole((256, 256)),
        ),
        compiler_params=params(),
        name="through",
    )(idx, pairs, *links)


def lower_kernel(idx, g_ref, m_ref, add_ref, out_ref):
    acc = add_ref[...]
    for s in range(4):
        halves = [m_ref[:, :, 2 * s + h].reshape(512, 128) for h in range(2)]
        cols = jnp.concatenate(halves, axis=1)
        acc += jnp.dot(g_ref[idx[8 + s]], cols, preferred_element_type=F32)
    out_ref[...] = (-acc.T).astype(BF16)


def lower(idx, g_own, m_two, add):
    return pl.pallas_call(
        lower_kernel,
        out_shape=jax.ShapeDtypeStruct((256, 256), BF16),
        grid_spec=pltpu.PrefetchScalarGridSpec(
            num_scalar_prefetch=1,
            grid=(1,),
            in_specs=[
                whole((8, 256, 512)),
                whole((8, 4, 8, 16, 128)),
                whole((256, 256)),
            ],
            out_specs=whole((256, 256)),
        ),
        compiler_params=params(),
        cost_estimate=pl.CostEstimate(
            flops=2 * 256 * 2048 * 256, bytes_accessed=3 * 1024 * 1024, transcendentals=0
        ),
        name="lower",
    )(idx, g_own, m_two, add)


def settle_kernel(dinv_ref, parts_ref, out_ref):
    total = jnp.sum(parts_ref[...].astype(F32), axis=0)
    out_ref[...] = (dinv_ref[...].astype(F32) - total).astype(BF16)


def settle(dinv, parts):
    return pl.pallas_call(
        settle_kernel,
        out_shape=jax.ShapeDtypeStruct((16, 128), BF16),
        compiler_params=params(),
        name="settle",
    )(dinv, parts)


def per_device(ginv_top, panel_one, panel_two, parent_link, dinv_one, struct_one, struct_two):
    r = lax.axis_index(ROW)
    c = lax.axis_index(COL)
    z = lax.axis_index("z")
    member = lax.axis_index(GROUP)
    list_one = lax.dynamic_index_in_dim(struct_one, r // 4, 0, keepdims=False)
    list_two = lax.dynamic_index_in_dim(struct_two, r // 2, 0, keepdims=False)
    own = list_one == c // 2
    place_two = jnp.argmax(list_one[None, :] == list_two[:, None], axis=1)
    here = jnp.stack([z, c % 2, jnp.argmax(own), jnp.any(own), member])
    idx = jnp.concatenate(
        [list_one, place_two.astype(jnp.int32), here.astype(jnp.int32), list_two]
    )

    g_all = lax.all_gather(ginv_top, ROW, axis=0, tiled=False)

    slots = jnp.concatenate(
        [panel_one.reshape(16, 16, 128), panel_two.reshape(16, 16, 256)], axis=2
    ).transpose(1, 0, 2)
    mine = lax.all_to_all(slots, ROW, 0, 0)

    packed = pack(idx, mine)
    across = lax.all_gather(packed, "yhi", axis=0, tiled=False)
    up_block, down_block = across[:, :8], across[:, 8:]
    copies = jnp.broadcast_to(up_block, (8, 4, 8, 16, 128))

    copies, parent_link = lax.optimization_barrier((copies, parent_link))
    m_one = lax.all_to_all(copies, "z", 0, 0)
    links = []
    for m in range(4):
        to = jnp.bitwise_xor(member, m)
        link = lax.dynamic_slice_in_dim(parent_link, to * 256, 256, 1)
        if m:
            link = lax.ppermute(link, GROUP, [(i, i ^ m) for i in range(4)])
        links.append(link)
    g_all, down_block, *links = lax.optimization_barrier((g_all, down_block, *links))
    m_two = lax.all_gather(down_block, "z", axis=0, tiled=False)
    g_own = choose(idx, g_all)
    m_one, g_own = lax.optimization_barrier((m_one, g_own))

    mine_one = upper(idx, g_own, m_one)
    pairs = lax.all_gather(mine_one, GROUP, axis=0, tiled=False)
    part = cross(pairs, mine_one)
    parts = lax.all_to_all(part.reshape(32, 16, 128), COL, 0, 0)
    diag_one = settle(dinv_one, parts)

    ginv_two = lower(idx, g_own, m_two, through(idx, pairs, links))
    return (mine_one[0], diag_one, ginv_two)


def solution(mesh):
    fine = Mesh(mesh.devices.reshape(2, 2, 2, 2, 8, 4), ROW + COL)
    return jax.shard_map(
        per_device,
        mesh=fine,
        in_specs=(
            P(COL, ROW),
            P(ROW + COL, None),
            P(ROW + COL, None),
            P(ROW, None),
            P(COL, ROW),
            P(),
            P(),
        ),
        out_specs=(P(COL, ROW), P(COL, ROW), P(ROW, COL)),
        check_vma=False,
    )
```

```python
import functools

import jax
import jax.numpy as jnp
from jax import lax
from jax.experimental import pallas as pl
from jax.experimental.pallas import tpu as pltpu
from jax.sharding import Mesh, PartitionSpec as P

ROW = ("ylo", "xh", "xl", "core")
COL = ("z", "yhi")
GROUP = ("xl", "core")
F32 = jnp.float32
BF16 = jnp.bfloat16
VMEM_LIMIT = 24 * 1024 * 1024


def params():
    return pltpu.CompilerParams(vmem_limit_bytes=VMEM_LIMIT)


def pack_kernel(idx, x_ref, out_ref):
    for s in range(8):
        out_ref[s] = x_ref[idx[s], :, 0:128]
    for s in range(4):
        block = idx[17 + s]
        out_ref[8 + 2 * s] = x_ref[block, :, 128:256]
        out_ref[9 + 2 * s] = x_ref[block, :, 256:384]


def pack(idx, x):
    return pl.pallas_call(
        pack_kernel,
        out_shape=jax.ShapeDtypeStruct((16, 16, 128), BF16),
        grid_spec=pltpu.PrefetchScalarGridSpec(
            num_scalar_prefetch=1,
            grid=(1,),
            in_specs=[pl.BlockSpec((16, 16, 384), lambda i, idx: (0, 0, 0))],
            out_specs=pl.BlockSpec((16, 16, 128), lambda i, idx: (0, 0, 0)),
        ),
        compiler_params=params(),
        name="pack",
    )(idx, x)


def choose_kernel(idx, g_ref, out_ref, sem):
    copies = [pltpu.make_async_copy(g_ref.at[idx[s]], out_ref.at[s], sem.at[s]) for s in range(8)]
    for copy in copies:
        copy.start()
    for copy in copies:
        copy.wait()


def choose(idx, g_all):
    return pl.pallas_call(
        choose_kernel,
        out_shape=jax.ShapeDtypeStruct((8, 256, 512), BF16),
        grid_spec=pltpu.PrefetchScalarGridSpec(
            num_scalar_prefetch=1,
            grid=(1,),
            in_specs=[pl.BlockSpec(memory_space=pl.ANY)],
            out_specs=pl.BlockSpec(memory_space=pl.ANY),
            scratch_shapes=[pltpu.SemaphoreType.DMA((8,))],
        ),
        compiler_params=params(),
        name="choose",
    )(idx, g_all)


def whole(shape):
    return pl.BlockSpec(shape, lambda i, idx: (0,) * len(shape))


def upper_kernel(idx, g_ref, m_ref, out_ref):
    rows = m_ref[pl.ds(idx[13] * 4, 4), :, idx[14]].reshape(256, 128)
    out_ref[1] = jnp.where(idx[15] > 0, rows, jnp.zeros_like(rows))
    acc = jnp.zeros((256, 128), F32)
    for s in range(8):
        cols = m_ref[:, :, s].reshape(512, 128)
        acc += jnp.dot(g_ref[s], cols, preferred_element_type=F32)
    out_ref[0] = (-acc).astype(BF16)


def upper(idx, g_own, m_one):
    return pl.pallas_call(
        upper_kernel,
        out_shape=jax.ShapeDtypeStruct((2, 256, 128), BF16),
        grid_spec=pltpu.PrefetchScalarGridSpec(
            num_scalar_prefetch=1,
            grid=(1,),
            in_specs=[whole((8, 256, 512)), whole((8, 4, 8, 16, 128))],
            out_specs=whole((2, 256, 128)),
        ),
        compiler_params=params(),
        cost_estimate=pl.CostEstimate(
            flops=2 * 256 * 4096 * 128, bytes_accessed=3 * 1024 * 1024, transcendentals=0
        ),
        name="upper",
    )(idx, g_own, m_one)


def cross_kernel(pair_ref, mine_ref, part_ref):
    gone = mine_ref[0]
    for h in range(4):
        part = lax.dot_general(
            pair_ref[h, 1], gone, (((0,), (0,)), ((), ())), preferred_element_type=F32
        )
        part_ref[pl.ds(h * 128, 128), :] = part.astype(BF16)


def cross(pairs, mine):
    return pl.pallas_call(
        cross_kernel,
        out_shape=jax.ShapeDtypeStruct((512, 128), BF16),
        compiler_params=params(),
        name="cross",
    )(pairs, mine)


def through_kernel(idx, pair_ref, l0, l1, l2, l3, out_ref):
    member = idx[16]
    acc = jnp.zeros((256, 256), F32)
    for m, link in enumerate((l0, l1, l2, l3)):
        gone = pair_ref[jnp.bitwise_xor(member, m), 0]
        acc += jnp.dot(gone, link[...], preferred_element_type=F32)
    out_ref[...] = acc


def through(idx, pairs, links):
    return pl.pallas_call(
        through_kernel,
        out_shape=jax.ShapeDtypeStruct((256, 256), F32),
        grid_spec=pltpu.PrefetchScalarGridSpec(
            num_scalar_prefetch=1,
            grid=(1,),
            in_specs=[whole((4, 2, 256, 128))] + [whole((128, 256))] * 4,
            out_specs=whole((256, 256)),
        ),
        compiler_params=params(),
        name="through",
    )(idx, pairs, *links)


def lower_kernel(idx, g_ref, m_ref, add_ref, out_ref):
    acc = add_ref[...]
    for s in range(4):
        halves = [m_ref[:, :, 2 * s + h].reshape(512, 128) for h in range(2)]
        cols = jnp.concatenate(halves, axis=1)
        acc += jnp.dot(g_ref[idx[8 + s]], cols, preferred_element_type=F32)
    out_ref[...] = (-acc.T).astype(BF16)


def lower(idx, g_own, m_two, add):
    return pl.pallas_call(
        lower_kernel,
        out_shape=jax.ShapeDtypeStruct((256, 256), BF16),
        grid_spec=pltpu.PrefetchScalarGridSpec(
            num_scalar_prefetch=1,
            grid=(1,),
            in_specs=[
                whole((8, 256, 512)),
                whole((8, 4, 8, 16, 128)),
                whole((256, 256)),
            ],
            out_specs=whole((256, 256)),
        ),
        compiler_params=params(),
        cost_estimate=pl.CostEstimate(
            flops=2 * 256 * 2048 * 256, bytes_accessed=3 * 1024 * 1024, transcendentals=0
        ),
        name="lower",
    )(idx, g_own, m_two, add)


def settle_kernel(dinv_ref, parts_ref, out_ref):
    total = jnp.sum(parts_ref[...].astype(F32), axis=0)
    out_ref[...] = (dinv_ref[...].astype(F32) - total).astype(BF16)


def settle(dinv, parts):
    return pl.pallas_call(
        settle_kernel,
        out_shape=jax.ShapeDtypeStruct((16, 128), BF16),
        compiler_params=params(),
        name="settle",
    )(dinv, parts)


def per_device(ginv_top, panel_one, panel_two, parent_link, dinv_one, struct_one, struct_two):
    r = lax.axis_index(ROW)
    c = lax.axis_index(COL)
    z = lax.axis_index("z")
    member = lax.axis_index(GROUP)
    list_one = lax.dynamic_index_in_dim(struct_one, r // 4, 0, keepdims=False)
    list_two = lax.dynamic_index_in_dim(struct_two, r // 2, 0, keepdims=False)
    own = list_one == c // 2
    place_two = jnp.argmax(list_one[None, :] == list_two[:, None], axis=1)
    here = jnp.stack([z, c % 2, jnp.argmax(own), jnp.any(own), member])
    idx = jnp.concatenate(
        [list_one, place_two.astype(jnp.int32), here.astype(jnp.int32), list_two]
    )

    g_all = lax.all_gather(ginv_top, ROW, axis=0, tiled=False)

    slots = jnp.concatenate(
        [panel_one.reshape(16, 16, 128), panel_two.reshape(16, 16, 256)], axis=2
    ).transpose(1, 0, 2)
    mine = lax.all_to_all(slots, ROW, 0, 0)

    packed = pack(idx, mine)
    across = lax.all_gather(packed, "yhi", axis=0, tiled=False)
    up_block, down_block = across[:, :8], across[:, 8:]
    copies = jnp.broadcast_to(up_block, (8, 4, 8, 16, 128))

    m_one = lax.all_to_all(copies, "z", 0, 0)
    g_all, down_block, parent_link = lax.optimization_barrier((g_all, down_block, parent_link))
    m_two = lax.all_gather(down_block, "z", axis=0, tiled=False)
    links = []
    for m in range(4):
        to = jnp.bitwise_xor(member, m)
        link = lax.dynamic_slice_in_dim(parent_link, to * 256, 256, 1)
        if m:
            link = lax.ppermute(link, GROUP, [(i, i ^ m) for i in range(4)])
        links.append(link)
    g_own = choose(idx, g_all)
    m_one, g_own, *links = lax.optimization_barrier((m_one, g_own, *links))

    mine_one = upper(idx, g_own, m_one)
    pairs = lax.all_gather(mine_one, GROUP, axis=0, tiled=False)
    part = cross(pairs, mine_one)
    parts = lax.all_to_all(part.reshape(32, 16, 128), COL, 0, 0)
    diag_one = settle(dinv_one, parts)

    ginv_two = lower(idx, g_own, m_two, through(idx, pairs, links))
    return (mine_one[0], diag_one, ginv_two)


def solution(mesh):
    fine = Mesh(mesh.devices.reshape(2, 2, 2, 2, 8, 4), ROW + COL)
    return jax.shard_map(
        per_device,
        mesh=fine,
        in_specs=(
            P(COL, ROW),
            P(ROW + COL, None),
            P(ROW + COL, None),
            P(ROW, None),
            P(COL, ROW),
            P(),
            P(),
        ),
        out_specs=(P(COL, ROW), P(COL, ROW), P(ROW, COL)),
        check_vma=False,
    )
```
